128 devices in a mesh: samp: 16 (over z, x), state: 8 (over y, core).
Axes of the slice: x: 4, y: 4, z: 4, core: 2. Of those that a mesh axis runs over, the one named last changes fastest.
Arguments:
- energies: bfloat16 [4096, 262144], P('state', 'samp'), may hold values from -12 to 12
- offsets: float32 [4096, 2048], P('state', 'samp'), may hold values from -250 to 250
- counts: int32 [4096], P('state'), may hold values from 1 to 64513, as said below
- labels: int32 [262144], P('samp'), may hold values from 0 to 4095
Outputs:
- free_energy: float32 [4096], P('state')
- own_log_probability: float32 [262144], P('samp')
The draws below stay inside these ranges and needn't reach their ends.
Inputs may be any that keep to these rules, and one draw needn't show every extreme that they name: counts[k] is the number of samples n with labels[n] = k; every state has a sample, state 4096 - 1 has exactly one, and state 0 has the most.
All inputs are finite; a program needn't handle non-finite values.
Results may differ from the reference program's by a relative error of at most 0.0003.
Values sent between devices are 32-bit elements; how exact they have to be, the bound alone decides.
No kernel may reach another device: no remote copies, remote signals or barrier semaphores. Data moves between devices by JAX's collectives and lax.ppermute only.
A program may use at most 192 MiB of HBM per device.

```python
import jax
import jax.numpy as jnp
from jax import lax

STATES = 4096
BLOCK = 128
ITERS = 3
SAMPLES = 262144


def labels_and_counts(key):
    base = jax.random.fold_in(key, 4711)
    first, second, third = jax.random.split(base, 3)
    extra = SAMPLES - STATES
    reserved = extra // 4
    picks = jnp.minimum(jax.random.randint(first, (extra,), 1, STATES - 1), jax.random.randint(second, (extra,), 1, STATES - 1))
    picks = jnp.where(jnp.arange(extra, dtype=jnp.int32) < reserved, 0, picks).astype(jnp.int32)
    allof = jnp.concatenate([jnp.arange(STATES, dtype=jnp.int32), picks])
    order = jax.random.permutation(third, SAMPLES)
    labels = allof[order].astype(jnp.int32)
    counts = jax.ops.segment_sum(jnp.ones((SAMPLES,), jnp.int32), labels, num_segments=STATES)
    return (labels, counts.astype(jnp.int32))


def draw_labels(key, part):
    return labels_and_counts(key)[0]


def draw_counts(key, part):
    return labels_and_counts(key)[1]


def draw_offsets(key, part):
    first = jax.random.fold_in(jax.random.fold_in(key, 99), 0)
    nblk = SAMPLES // BLOCK
    rough = 2.0 * jnp.clip(jax.random.normal(first, (STATES, nblk), jnp.float32), -6.0, 6.0)
    return rough


def levels(key, shape, cuts, smallest, largest):
    level, own = 1.0, jax.random.fold_in(key, 6)
    for dim, blocks in cuts:
        steps = jnp.exp(jax.random.uniform(jax.random.fold_in(own, dim), (blocks,), jnp.float32, smallest / len(cuts), largest / len(cuts)))
        level = level * jnp.repeat(steps, shape[dim] // blocks).reshape([-1 if axis == dim else 1 for axis in range(len(shape))])
    return level


def noise(rng, dims, scale, reach, pieces=(), kind=jnp.bfloat16):
    level = levels(rng, dims, pieces, -0.22, 0.18) if pieces else 1.0
    entries = jax.random.normal(rng, dims, jnp.float32) * scale * level
    return jnp.minimum(jnp.maximum(entries, -reach), reach).astype(kind)


def setup_inputs(seed: int = 0) -> dict:
    streams_of = jax.random.split(jax.random.key(seed), 5)
    return {
        "energies": noise(streams_of[0], (STATES, SAMPLES), 2.0, 12.0, ((0, 8), (1, 16))),
        "offsets": draw_offsets(jax.random.fold_in(streams_of[4], 71), 0),
        "counts": draw_counts(jax.random.fold_in(streams_of[4], 71), 0),
        "labels": draw_labels(jax.random.fold_in(streams_of[4], 71), 0),
    }


def energy_rows(energies, offsets, start, rows):
    part = lax.dynamic_slice_in_dim(energies, start, rows, 0).astype(jnp.float32)
    shift = lax.dynamic_slice_in_dim(offsets, start, rows, 0)
    nblk = offsets.shape[1]
    return (part.reshape(rows, nblk, BLOCK) + shift[:, :, None]).reshape(rows, nblk * BLOCK)


def denominator(energies, offsets, logc, free):
    rows = min(256, STATES)
    count = STATES // rows

    def step(carry, index):
        best, total = carry
        start = (index * rows).astype(jnp.int32)
        u = energy_rows(energies, offsets, start, rows)
        lead = lax.dynamic_slice_in_dim(logc + free, start, rows, 0)
        terms = lead[:, None] - u
        newbest = jnp.maximum(best, jnp.max(terms, axis=0))
        total = total * jnp.exp(best - newbest) + jnp.sum(jnp.exp(terms - newbest[None, :]), axis=0)
        return (newbest, total), None

    init = (jnp.full((SAMPLES,), -1e30, jnp.float32), jnp.zeros((SAMPLES,), jnp.float32))
    (best, total), _ = lax.scan(step, init, jnp.arange(count, dtype=jnp.int32))
    return best + jnp.log(total)


def update(energies, offsets, denom):
    rows = min(256, STATES)
    count = STATES // rows

    def one(index):
        start = (index * rows).astype(jnp.int32)
        terms = -energy_rows(energies, offsets, start, rows) - denom[None, :]
        best = jnp.max(terms, axis=1)
        return -(best + jnp.log(jnp.sum(jnp.exp(terms - best[:, None]), axis=1)))

    return lax.map(one, jnp.arange(count, dtype=jnp.int32)).reshape(STATES)


def reference(energies, offsets, counts, labels):
    logc = jnp.log(counts.astype(jnp.float32))
    free = jnp.zeros((STATES,), jnp.float32)
    for step in range(ITERS):
        denom = denominator(energies, offsets, logc, free)
        free = update(energies, offsets, denom)
    denom = denominator(energies, offsets, logc, free)
    picked = jnp.take_along_axis(energies, labels[None, :], axis=0)[0].astype(jnp.float32)
    blocks = (jnp.arange(SAMPLES, dtype=jnp.int32) // BLOCK).astype(jnp.int32)
    picked = picked + offsets[labels, blocks]
    own = logc[labels] + free[labels] - picked - denom
    return free - free[0], own
```

```python
import functools

import jax
import jax.numpy as jnp
from jax import lax
from jax.experimental import pallas as pl
from jax.experimental.pallas import tpu as pltpu
from jax.sharding import PartitionSpec as P

ITERS = 3
LANES = 128
GROUP = 8
PIECES = 2
VMEM = pltpu.VMEM
WHOLE = pl.BlockSpec(memory_space=pltpu.VMEM)


def params(mib):
    return pltpu.CompilerParams(vmem_limit_bytes=mib << 20)


def block_weights(lead, offt_ref, w_ref, top_ref):
    h = lead - offt_ref[...]
    top = jnp.max(h, axis=1, keepdims=True)
    top_ref[...] = jnp.broadcast_to(top, top_ref.shape)
    w_ref[...] = jnp.exp(h - top)


def spread(ref, g, j, q):
    tile = ref[pl.ds(pl.multiple_of(g * GROUP, GROUP), GROUP), q * LANES : (q + 1) * LANES]
    return jnp.broadcast_to(tile[j : j + 1, :], (8, LANES))


def row_sums(load, w_ref, g, j, acc, rows):
    lane = lax.broadcasted_iota(jnp.int32, (8, acc[0].shape[1]), 1)
    here = lane == g * GROUP + j
    nq = w_ref.shape[1] // LANES
    w = [spread(w_ref, g, j, q) for q in range(nq)]
    out = []
    for i in range(rows // 8):
        total = load(i, 0) * w[0]
        for q in range(1, nq):
            total = total + load(i, q) * w[q]
        col = jnp.sum(total, axis=1, keepdims=True)
        out.append(jnp.where(here, col, acc[i]))
    return tuple(out)


def log_rows(acc, top_ref):
    return top_ref[...] + jnp.log(jnp.concatenate(acc, axis=0).T)


def over_pieces(step, ex_refs, steps, carry):
    each = steps // len(ex_refs)
    for p, ex_ref in enumerate(ex_refs):
        carry = lax.fori_loop(p * each, (p + 1) * each, functools.partial(step, ex_ref, p * each), carry)
    return carry


def prep_kernel(e_hbm, off_ref, counts_ref, labels_ref, mine_ref, *refs):
    ex_refs, (offt_ref, out_ref, local_ref, root_ref, buf, sem, w_ref, top_ref) = refs[:PIECES], refs[PIECES:]
    rows = LANES
    nk = buf.shape[1]
    nq = nk // LANES
    span = buf.shape[2]
    steps = e_hbm.shape[1] // span

    def copy(step, slot):
        at = pl.multiple_of(step * span, span)
        return pltpu.make_async_copy(e_hbm.at[:, pl.ds(at, span)], buf.at[slot], sem.at[slot])

    copy(0, 0).start()
    mine = mine_ref[...]
    local_ref[...] = labels_ref[...] - mine * nk
    root_ref[...] = (mine == 0).astype(jnp.int32)
    offt_ref[...] = off_ref[...].T
    block_weights(jnp.log(counts_ref[...].astype(jnp.float32)), offt_ref, w_ref, top_ref)

    def step(ex_ref, first, g, acc):
        slot = lax.rem(g, 2)

        @pl.when(g + 1 < steps)
        def _():
            copy(g + 1, 1 - slot).start()

        copy(g, slot).wait()
        for j in range(span // rows):
            base = pl.multiple_of((g - first) * span + j * rows, rows)
            for q in range(nq):
                tile = buf[slot, q * LANES : (q + 1) * LANES, j * rows : (j + 1) * rows]
                ex_ref[pl.ds(base, rows), q * LANES : (q + 1) * LANES] = jnp.exp(
                    -(tile.astype(jnp.float32).T)
                )

            def load(i, q, base=base):
                return ex_ref[pl.ds(base + i * 8, 8), q * LANES : (q + 1) * LANES]

            acc = row_sums(load, w_ref, g, j, acc, rows)
        return acc

    acc = (jnp.zeros((8, out_ref.shape[0]), jnp.float32),) * (rows // 8)
    acc = over_pieces(step, ex_refs, steps, acc)
    out_ref[...] = log_rows(acc, top_ref)


def prep(energies, offsets, counts, labels, mine):
    nk, width = energies.shape
    nblk = offsets.shape[1]
    span = GROUP * LANES
    return pl.pallas_call(
        prep_kernel,
        out_shape=(pltpu.VMEM((width // PIECES, nk), jnp.float32),) * PIECES + (
            jax.ShapeDtypeStruct((nblk, nk), jnp.float32),
            jax.ShapeDtypeStruct((nblk, LANES), jnp.float32),
            jax.ShapeDtypeStruct(labels.shape, jnp.int32),
            jax.ShapeDtypeStruct((1, 1), jnp.int32),
        ),
        in_specs=[pl.BlockSpec(memory_space=pl.ANY)] + [WHOLE] * 4,
        out_specs=(WHOLE,) * (PIECES + 4),
        scratch_shapes=[
            pltpu.VMEM((2, nk, span), jnp.bfloat16),
            pltpu.SemaphoreType.DMA((2,)),
            pltpu.VMEM((nblk, nk), jnp.float32),
            pltpu.VMEM((nblk, LANES), jnp.float32),
        ],
        compiler_params=params(12),
        name="prep",
    )(energies, offsets, counts, labels, mine)


def pick_kernel(e_ref, label_ref, _, out_ref):
    nk, span = e_ref.shape
    kid = lax.broadcasted_iota(jnp.int32, (16, LANES), 0)
    for j in range(span // LANES):
        want = jnp.broadcast_to(label_ref[j : j + 1, :], (16, LANES))
        acc = jnp.zeros((16, LANES), jnp.float32)
        for k in range(nk // 16):
            tile = e_ref[k * 16 : (k + 1) * 16, j * LANES : (j + 1) * LANES].astype(jnp.float32)
            acc = jnp.where(want == kid + k * 16, tile, acc)
        out_ref[j : j + 1, :] = jnp.sum(acc, axis=0, keepdims=True)


def pick(energies, local_label, after):
    nk, width = energies.shape
    span = GROUP * LANES
    return pl.pallas_call(
        pick_kernel,
        grid=(width // span,),
        out_shape=jax.ShapeDtypeStruct(local_label.shape, jnp.float32),
        in_specs=[
            pl.BlockSpec((nk, span), lambda i: (0, i)),
            pl.BlockSpec((GROUP, LANES), lambda i: (i, 0)),
            pl.BlockSpec(memory_space=pl.ANY),
        ],
        out_specs=pl.BlockSpec((GROUP, LANES), lambda i: (i, 0)),
        compiler_params=params(8),
        cost_estimate=pl.CostEstimate(flops=width * nk * 3, bytes_accessed=width * nk * 2, transcendentals=0),
        name="pick",
    )(pltpu.with_memory_space_constraint(energies, pltpu.HBM), local_label, after)


def lse(values):
    best = functools.reduce(jnp.maximum, values)
    return best + jnp.log(sum(jnp.exp(v - best) for v in values))


def update_kernel(n_in, *refs):
    parts, ex_refs, offt_ref = refs[:n_in], refs[n_in : n_in + PIECES], refs[n_in + PIECES]
    out_ref, vt_ref, g_ref = refs[-3:]
    nblk, nk = offt_ref.shape
    nq = nk // LANES
    d = lse([p[...] for p in parts])
    low = jnp.min(d, axis=1, keepdims=True)
    vt_ref[...] = jnp.exp(low - d).T
    h = -offt_ref[...] - low
    top = jnp.max(h, axis=0, keepdims=True)
    g_ref[...] = jnp.exp(h - top)

    def step(ex_ref, first, g, total):
        cols = [
            pltpu.roll(vt_ref[i * 8 : (i + 1) * 8, :], lax.rem(nblk - g * GROUP, nblk), 1)
            for i in range(LANES // 8)
        ]
        for j in range(GROUP):
            acc = [None] * nq
            for i in range(LANES // 8):
                v = jnp.broadcast_to(cols[i][:, j : j + 1], (8, LANES))
                at = pl.multiple_of(((g - first) * GROUP + j) * LANES + i * 8, 8)
                for q in range(nq):
                    term = ex_ref[pl.ds(at, 8), q * LANES : (q + 1) * LANES] * v
                    acc[q] = term if acc[q] is None else acc[q] + term
            total = tuple(
                total[q] + acc[q] * spread(g_ref, g, j, q)
                for q in range(nq)
            )
        return total

    zero = jnp.zeros((8, LANES), jnp.float32)
    total = over_pieces(step, ex_refs, nblk // GROUP, (zero,) * nq)
    sums = jnp.concatenate([jnp.sum(t, axis=0, keepdims=True) for t in total], axis=1)
    out_ref[...] = jnp.broadcast_to((top + jnp.log(sums))[None], out_ref.shape)


def update(parts, ex, offt, copies, after=()):
    nblk, nk = offt.shape
    return pl.pallas_call(
        functools.partial(update_kernel, len(parts)),
        out_shape=jax.ShapeDtypeStruct((copies, 1, nk), jnp.float32),
        in_specs=[WHOLE] * (len(parts) + PIECES + 1) + [pl.BlockSpec(memory_space=pl.ANY)] * len(after),
        out_specs=WHOLE,
        scratch_shapes=[pltpu.VMEM((LANES, nblk), jnp.float32), pltpu.VMEM((nblk, nk), jnp.float32)],
        compiler_params=params(8),
        name="update",
    )(*parts, *(pltpu.with_memory_space_constraint(e, VMEM) for e in ex), offt, *after)


def denom_sums(free, counts_ref, ex_refs, offt_ref, w_ref, top_ref):
    nblk = offt_ref.shape[0]
    lead = jnp.log(counts_ref[...].astype(jnp.float32)) + free
    block_weights(lead, offt_ref, w_ref, top_ref)

    def step(ex_ref, first, g, acc):
        for j in range(GROUP):

            def load(i, q, j=j):
                at = pl.multiple_of(((g - first) * GROUP + j) * LANES + i * 8, 8)
                return ex_ref[pl.ds(at, 8), q * LANES : (q + 1) * LANES]

            acc = row_sums(load, w_ref, g, j, acc, LANES)
        return acc

    acc = (jnp.zeros((8, nblk), jnp.float32),) * (LANES // 8)
    acc = over_pieces(step, ex_refs, nblk // GROUP, acc)
    return lead, log_rows(acc, top_ref)


def free_of(gathered):
    best = jnp.max(gathered, axis=0, keepdims=True)
    total = jnp.sum(jnp.exp(gathered - best), axis=0, keepdims=True)
    return -(best + jnp.log(total))[0]


def denom_kernel(gathered_ref, counts_ref, *refs):
    ex_refs, (offt_ref, out_ref, w_ref, top_ref) = refs[:PIECES], refs[PIECES:]
    free = free_of(gathered_ref[...])
    out_ref[...] = denom_sums(free, counts_ref, ex_refs, offt_ref, w_ref, top_ref)[1]


def last_kernel(gathered_ref, counts_ref, *refs):
    ex_refs, (offt_ref, label_ref, picked_ref, root_ref, out_ref, free_ref, w_ref, top_ref) = refs[:PIECES], refs[PIECES:]
    nblk, nk = offt_ref.shape
    free = free_of(gathered_ref[...])
    free_ref[...] = free
    lead, sums = denom_sums(free, counts_ref, ex_refs, offt_ref, w_ref, top_ref)
    out_ref[0:nblk, :] = sums
    for r in range(nblk // 8):
        at = slice(r * 8, (r + 1) * 8)
        label = label_ref[at, :]
        low = label & (LANES - 1)
        high = label >> 7
        own = jnp.zeros((8, LANES), jnp.float32)
        for q in range(nk // LANES):
            cut = slice(q * LANES, (q + 1) * LANES)
            table = lead[:, cut] - offt_ref[at, cut]
            value = jnp.take_along_axis(table, low, axis=1, mode="promise_in_bounds")
            own = jnp.where(high == q, value - picked_ref[at, :], own)
        out_ref[nblk + r * 8 : nblk + (r + 1) * 8, :] = own
    anchor = jnp.where(root_ref[...] == 1, free[0:1, 0:1], 0.0)
    out_ref[2 * nblk : 2 * nblk + 8, :] = jnp.broadcast_to(anchor, (8, LANES))


def denom(gathered, counts, ex, offt, extra=()):
    nblk, nk = offt.shape
    rows = jax.ShapeDtypeStruct((nblk, LANES), jnp.float32)
    if extra:
        rows = (
            jax.ShapeDtypeStruct((2 * nblk + 8, LANES), jnp.float32),
            jax.ShapeDtypeStruct((1, nk), jnp.float32),
        )
    return pl.pallas_call(
        last_kernel if extra else denom_kernel,
        out_shape=rows,
        in_specs=[WHOLE] * (3 + PIECES + len(extra)),
        out_specs=(WHOLE, WHOLE) if extra else WHOLE,
        scratch_shapes=[pltpu.VMEM((nblk, nk), jnp.float32), pltpu.VMEM((nblk, LANES), jnp.float32)],
        compiler_params=params(8),
        name="last" if extra else "denom",
    )(gathered, counts, *(pltpu.with_memory_space_constraint(e, VMEM) for e in ex), offt, *extra)


def pair_kernel(a_ref, b_ref, out_ref):
    rows = LANES
    out_ref[0:rows, :] = lse([a_ref[0:rows, :], b_ref[0:rows, :]])
    if out_ref.shape[0] > rows:
        out_ref[rows:, :] = a_ref[rows:, :] + b_ref[rows:, :]


def paired(value, size):
    return pl.pallas_call(
        pair_kernel,
        out_shape=jax.ShapeDtypeStruct(value.shape, value.dtype),
        in_specs=[WHOLE] * 2,
        out_specs=WHOLE,
        compiler_params=params(4),
        name="pair",
    )(value, partner(value, size))


def shift_state(value, size, move):
    return lax.ppermute(value, "state", [(i, move(i)) for i in range(size)])


def partner(value, size):
    return shift_state(value, size, lambda i: i ^ 1)


def others(value, size):
    return [
        shift_state(value, size, lambda i, d=d: (i + 2 * d) % size) for d in range(1, size // 2)
    ]


def shards(samp, state, energies, offsets, counts, labels):
    nk, width = energies.shape
    nblk = offsets.shape[1]
    mine = jnp.broadcast_to(lax.axis_index("state"), (1, 1)).astype(jnp.int32)
    counts_row = counts.reshape(1, nk)
    *ex, offt, sums, local_label, root = prep(
        energies, offsets, counts_row, labels.reshape(nblk, width // nblk), mine
    )
    picked = None
    for step in range(ITERS):
        pair = paired(sums, state)
        parts = [pair, *others(pair, state)]
        if picked is None:
            picked = pick(energies, local_label, pair)
            out = update(parts, ex, offt, samp, (picked,))
        else:
            out = update(parts, ex, offt, samp)
        gathered = lax.all_to_all(out, "samp", 0, 0, tiled=True)
        if step < ITERS - 1:
            sums = denom(gathered, counts_row, ex, offt)
    both, free = denom(gathered, counts_row, ex, offt, (local_label, picked, root))
    pair = paired(both, state)
    parts = [pair, *others(pair, state)]
    d = lse([p[:nblk] for p in parts])
    rest = sum(p[nblk:] for p in parts)
    own = (rest[:nblk] - d).reshape(width)
    return (free - rest[nblk : nblk + 1, 0:1]).reshape(nk), own


def solution(mesh):
    return jax.shard_map(
        functools.partial(shards, mesh.shape["samp"], mesh.shape["state"]),
        mesh=mesh,
        in_specs=(P("state", "samp"), P("state", "samp"), P("state"), P("samp")),
        out_specs=(P("state"), P("samp")),
        check_vma=False,
    )
```

```python
import functools

import jax
import jax.numpy as jnp
from jax import lax
from jax.experimental import pallas as pl
from jax.experimental.pallas import tpu as pltpu
from jax.sharding import PartitionSpec as P

ITERS = 3
LANES = 128
GROUP = 8
PIECES = 2
UNROLL_UPDATE = 1
UNROLL_DENOM = 8
VMEM = pltpu.VMEM
WHOLE = pl.BlockSpec(memory_space=pltpu.VMEM)


def params(mib):
    return pltpu.CompilerParams(vmem_limit_bytes=mib << 20)


def block_weights(lead, offt_ref, w_ref, top_ref):
    h = lead - offt_ref[...]
    top = jnp.max(h, axis=1, keepdims=True)
    top_ref[...] = jnp.broadcast_to(top, top_ref.shape)
    w_ref[...] = jnp.exp(h - top)


def spread(ref, g, j, q):
    tile = ref[pl.ds(pl.multiple_of(g * GROUP, GROUP), GROUP), q * LANES : (q + 1) * LANES]
    return jnp.broadcast_to(tile[j : j + 1, :], (8, LANES))


def row_sums(load, w_ref, g, j, acc, rows):
    lane = lax.broadcasted_iota(jnp.int32, (8, acc[0].shape[1]), 1)
    here = lane == g * GROUP + j
    nq = w_ref.shape[1] // LANES
    w = [spread(w_ref, g, j, q) for q in range(nq)]
    out = []
    for i in range(rows // 8):
        total = load(i, 0) * w[0]
        for q in range(1, nq):
            total = total + load(i, q) * w[q]
        col = jnp.sum(total, axis=1, keepdims=True)
        out.append(jnp.where(here, col, acc[i]))
    return tuple(out)


def log_rows(acc, top_ref):
    return top_ref[...] + jnp.log(jnp.concatenate(acc, axis=0).T)


def over_pieces(step, ex_refs, steps, carry, unroll=1):
    each = steps // len(ex_refs)
    for p, ex_ref in enumerate(ex_refs):
        carry = lax.fori_loop(p * each, (p + 1) * each, functools.partial(step, ex_ref, p * each), carry, unroll=unroll)
    return carry


def prep_kernel(e_hbm, off_hbm, counts_hbm, labels_hbm, mine_ref, *refs):
    ex_refs, outs = refs[:PIECES], refs[PIECES:]
    offt_ref, out_ref, local_ref, who_ref, counts_ref, buf, sem, off_ref, small_sem, w_ref, top_ref = outs
    nk, span = buf.shape[1:]
    depth = buf.shape[0]
    steps = e_hbm.shape[1] // span
    side = 2 * LANES
    nq = nk // LANES

    def copy(step, slot):
        at = pl.multiple_of(step * span, span)
        return pltpu.make_async_copy(e_hbm.at[:, pl.ds(at, span)], buf.at[slot], sem.at[slot])

    small = [
        pltpu.make_async_copy(src, dst, small_sem.at[n])
        for n, (src, dst) in enumerate(
            [(off_hbm, off_ref), (counts_hbm, counts_ref), (labels_hbm, local_ref)]
        )
    ]
    for c in small:
        c.start()
    for n in range(depth - 1):
        copy(n, n).start()
    eye = lax.broadcasted_iota(jnp.int32, (side, side), 0) == lax.broadcasted_iota(jnp.int32, (side, side), 1)
    minus = jnp.where(eye, -1.0, 0.0).astype(jnp.bfloat16)
    for c in small:
        c.wait()
    mine = mine_ref[...]
    local_ref[...] = local_ref[...] - mine * nk
    who_ref[...] = mine
    offt_ref[...] = off_ref[...].T
    block_weights(jnp.log(counts_ref[...].astype(jnp.float32)), offt_ref, w_ref, top_ref)

    def step(ex_ref, first, g, acc):
        slot = lax.rem(g, depth)

        @pl.when(g + depth - 1 < steps)
        def _():
            copy(g + depth - 1, lax.rem(g + depth - 1, depth)).start()

        copy(g, slot).wait()
        for c in range(span // side):
            base = pl.multiple_of((g - first) * span + c * side, side)
            pieces = []
            for q in range(nk // side):
                tile = buf[slot, q * side : (q + 1) * side, c * side : (c + 1) * side]
                turned = lax.dot_general(
                    minus, tile, (((1,), (1,)), ((), ())), preferred_element_type=jnp.float32
                )
                value = jnp.exp(turned)
                ex_ref[pl.ds(base, side), q * side : (q + 1) * side] = value
                pieces.append(value)

            for half in range(2):

                def load(i, q, half=half):
                    at = half * LANES + i * 8
                    lane = (q % 2) * LANES
                    return pieces[q // 2][at : at + 8, lane : lane + LANES]

                acc = row_sums(load, w_ref, g, 2 * c + half, acc, LANES)
        return acc

    acc = (jnp.zeros((8, out_ref.shape[0]), jnp.float32),) * (LANES // 8)
    acc = over_pieces(step, ex_refs, steps, acc)
    out_ref[...] = log_rows(acc, top_ref)


def prep(energies, offsets, counts, labels, mine):
    nk, width = energies.shape
    nblk = offsets.shape[1]
    span = GROUP * LANES
    depth = 4
    anywhere = pl.BlockSpec(memory_space=pl.ANY)
    return pl.pallas_call(
        prep_kernel,
        out_shape=(pltpu.VMEM((width // PIECES, nk), jnp.float32),) * PIECES + (
            jax.ShapeDtypeStruct((nblk, nk), jnp.float32),
            jax.ShapeDtypeStruct((nblk, LANES), jnp.float32),
            jax.ShapeDtypeStruct(labels.shape, jnp.int32),
            jax.ShapeDtypeStruct((1, 1), jnp.int32),
            jax.ShapeDtypeStruct((1, nk), jnp.int32),
        ),
        in_specs=[anywhere] * 4 + [WHOLE],
        out_specs=(WHOLE,) * (PIECES + 5),
        scratch_shapes=[
            pltpu.VMEM((depth, nk, span), jnp.bfloat16),
            pltpu.SemaphoreType.DMA((depth,)),
            pltpu.VMEM((nk, nblk), jnp.float32),
            pltpu.SemaphoreType.DMA((3,)),
            pltpu.VMEM((nblk, nk), jnp.float32),
            pltpu.VMEM((nblk, LANES), jnp.float32),
        ],
        compiler_params=params(12),
        name="prep",
    )(*(pltpu.with_memory_space_constraint(a, pltpu.HBM) for a in (energies, offsets, counts, labels)), mine)


def pick_kernel(e_ref, label_ref, _, out_ref):
    nk, span = e_ref.shape
    kid = lax.broadcasted_iota(jnp.int32, (16, LANES), 0).astype(jnp.int16)
    far = jnp.int32(-1)
    for j in range(span // LANES):
        label = label_ref[j : j + 1, :]
        label = jnp.where((label >= 0) & (label < nk), label, far)
        want = jnp.broadcast_to(label, (16, LANES)).astype(jnp.int16)
        acc = [jnp.zeros((16, LANES), jnp.bfloat16) for _ in range(2)]
        for k in range(nk // 16):
            tile = e_ref[k * 16 : (k + 1) * 16, j * LANES : (j + 1) * LANES]
            acc[k % 2] = jnp.where(want == kid + jnp.int16(k * 16), tile, acc[k % 2])
        both = acc[0].astype(jnp.float32) + acc[1].astype(jnp.float32)
        out_ref[j : j + 1, :] = jnp.sum(both, axis=0, keepdims=True)


def pick(energies, local_label, first, count, after):
    nk = energies.shape[0]
    span = GROUP * LANES
    return pl.pallas_call(
        pick_kernel,
        grid=(count,),
        out_shape=jax.ShapeDtypeStruct((count * GROUP, LANES), jnp.float32),
        in_specs=[
            pl.BlockSpec((nk, span), lambda i: (0, i + first)),
            pl.BlockSpec((GROUP, LANES), lambda i: (i + first, 0)),
            pl.BlockSpec(memory_space=pl.ANY),
        ],
        out_specs=pl.BlockSpec((GROUP, LANES), lambda i: (i, 0)),
        compiler_params=params(8),
        cost_estimate=pl.CostEstimate(
            flops=count * span * nk * 3, bytes_accessed=count * span * nk * 2, transcendentals=0
        ),
        name="pick",
    )(pltpu.with_memory_space_constraint(energies, pltpu.HBM), local_label, after)


def lse(values):
    best = functools.reduce(jnp.maximum, values)
    return best + jnp.log(sum(jnp.exp(v - best) for v in values))


def update_kernel(n_in, *refs):
    parts, ex_refs, offt_ref = refs[:n_in], refs[n_in : n_in + PIECES], refs[n_in + PIECES]
    out_ref, vt_ref, g_ref = refs[-3:]
    nblk, nk = offt_ref.shape
    nq = nk // LANES
    d = lse([p[...] for p in parts])
    low = jnp.min(d, axis=1, keepdims=True)
    turned = jnp.exp(low - d).T
    for g in range(nblk // GROUP):
        vt_ref[g * LANES : (g + 1) * LANES, :] = pltpu.roll(turned, (nblk - g * GROUP) % nblk, 1)
    h = -offt_ref[...] - low
    top = jnp.max(h, axis=0, keepdims=True)
    g_ref[...] = jnp.exp(h - top)

    def step(ex_ref, first, g, total):
        for j in range(GROUP):
            acc = [None] * nq
            for i in range(LANES // 8):
                col = vt_ref[pl.ds(pl.multiple_of(g * LANES + i * 8, 8), 8), :]
                v = jnp.broadcast_to(col[:, j : j + 1], (8, LANES))
                at = pl.multiple_of(((g - first) * GROUP + j) * LANES + i * 8, 8)
                for q in range(nq):
                    term = ex_ref[pl.ds(at, 8), q * LANES : (q + 1) * LANES] * v
                    acc[q] = term if acc[q] is None else acc[q] + term
            total = tuple(
                total[q] + acc[q] * spread(g_ref, g, j, q)
                for q in range(nq)
            )
        return total

    zero = jnp.zeros((8, LANES), jnp.float32)
    total = over_pieces(step, ex_refs, nblk // GROUP, (zero,) * nq, UNROLL_UPDATE)
    sums = jnp.concatenate([jnp.sum(t, axis=0, keepdims=True) for t in total], axis=1)
    out_ref[...] = jnp.broadcast_to((top + jnp.log(sums))[None], out_ref.shape)


def update(parts, ex, offt, copies, after=()):
    nblk, nk = offt.shape
    return pl.pallas_call(
        functools.partial(update_kernel, len(parts)),
        out_shape=jax.ShapeDtypeStruct((copies, 1, nk), jnp.float32),
        in_specs=[WHOLE] * (len(parts) + PIECES + 1) + [pl.BlockSpec(memory_space=pl.ANY)] * len(after),
        out_specs=WHOLE,
        scratch_shapes=[
            pltpu.VMEM((nblk // GROUP * LANES, nblk), jnp.float32),
            pltpu.VMEM((nblk, nk), jnp.float32),
        ],
        compiler_params=params(8),
        name="update",
    )(*parts, *(pltpu.with_memory_space_constraint(e, VMEM) for e in ex), offt, *after)


def denom_sums(free, counts_ref, ex_refs, offt_ref, w_ref, top_ref):
    nblk = offt_ref.shape[0]
    lead = jnp.log(counts_ref[...].astype(jnp.float32)) + free
    block_weights(lead, offt_ref, w_ref, top_ref)

    def step(ex_ref, first, g, acc):
        for j in range(GROUP):

            def load(i, q, j=j):
                at = pl.multiple_of(((g - first) * GROUP + j) * LANES + i * 8, 8)
                return ex_ref[pl.ds(at, 8), q * LANES : (q + 1) * LANES]

            acc = row_sums(load, w_ref, g, j, acc, LANES)
        return acc

    acc = (jnp.zeros((8, nblk), jnp.float32),) * (LANES // 8)
    acc = over_pieces(step, ex_refs, nblk // GROUP, acc, UNROLL_DENOM)
    return lead, log_rows(acc, top_ref)


def free_of(gathered):
    best = jnp.max(gathered, axis=0, keepdims=True)
    total = jnp.sum(jnp.exp(gathered - best), axis=0, keepdims=True)
    return -(best + jnp.log(total))[0]


def denom_kernel(gathered_ref, counts_ref, *refs):
    ex_refs, (offt_ref, out_ref, w_ref, top_ref) = refs[:PIECES], refs[PIECES:]
    free = free_of(gathered_ref[...])
    out_ref[...] = denom_sums(free, counts_ref, ex_refs, offt_ref, w_ref, top_ref)[1]


def last_kernel(gathered_ref, counts_ref, *refs):
    ex_refs, (offt_ref, label_ref, who_ref, *refs) = refs[:PIECES], refs[PIECES:]
    *picked_refs, keep_ref, send_ref, free_ref, w_ref, top_ref = refs
    picked = [ref[r * 8 : (r + 1) * 8, :] for ref in picked_refs for r in range(ref.shape[0] // 8)]
    nblk, nk = offt_ref.shape
    half = nblk // 2
    free = free_of(gathered_ref[...])
    free_ref[...] = free
    lead, sums = denom_sums(free, counts_ref, ex_refs, offt_ref, w_ref, top_ref)
    even = (who_ref[...] & 1) == 0
    keep_ref[0:half, :] = jnp.where(even, sums[:half], sums[half:])
    send_ref[0:half, :] = jnp.where(even, sums[half:], sums[:half])
    own = []
    for r in range(nblk // 8):
        at = slice(r * 8, (r + 1) * 8)
        label = label_ref[at, :]
        low = label & (LANES - 1)
        high = label >> 7
        term = jnp.zeros((8, LANES), jnp.float32)
        for q in range(nk // LANES):
            cut = slice(q * LANES, (q + 1) * LANES)
            table = lead[:, cut] - offt_ref[at, cut]
            value = jnp.take_along_axis(table, low, axis=1, mode="promise_in_bounds")
            term = jnp.where(high == q, value - picked[r], term)
        own.append(term)
    for r in range(half // 8):
        first, second = own[r], own[r + half // 8]
        at = slice(half + r * 8, half + (r + 1) * 8)
        keep_ref[at, :] = jnp.where(even, first, second)
        send_ref[at, :] = jnp.where(even, second, first)
    anchor = jnp.broadcast_to(jnp.where(who_ref[...] == 0, free[0:1, 0:1], 0.0), (8, LANES))
    keep_ref[nblk:, :] = anchor
    send_ref[nblk:, :] = anchor


def denom(gathered, counts, ex, offt, extra=()):
    nblk, nk = offt.shape
    rows = jax.ShapeDtypeStruct((nblk, LANES), jnp.float32)
    if extra:
        rows = (
            jax.ShapeDtypeStruct((nblk + 8, LANES), jnp.float32),
            jax.ShapeDtypeStruct((nblk + 8, LANES), jnp.float32),
            jax.ShapeDtypeStruct((1, nk), jnp.float32),
        )
    return pl.pallas_call(
        last_kernel if extra else denom_kernel,
        out_shape=rows,
        in_specs=[WHOLE] * (3 + PIECES + len(extra)),
        out_specs=(WHOLE,) * 3 if extra else WHOLE,
        scratch_shapes=[pltpu.VMEM((nblk, nk), jnp.float32), pltpu.VMEM((nblk, LANES), jnp.float32)],
        compiler_params=params(8),
        name="last" if extra else "denom",
    )(gathered, counts, *(pltpu.with_memory_space_constraint(e, VMEM) for e in ex), offt, *extra)


def pair_kernel(rows, a_ref, b_ref, out_ref):
    out_ref[0:rows, :] = lse([a_ref[0:rows, :], b_ref[0:rows, :]])
    if out_ref.shape[0] > rows:
        out_ref[rows:, :] = a_ref[rows:, :] + b_ref[rows:, :]


def paired(mine, theirs, rows):
    return pl.pallas_call(
        functools.partial(pair_kernel, rows),
        out_shape=jax.ShapeDtypeStruct(mine.shape, mine.dtype),
        in_specs=[WHOLE] * 2,
        out_specs=WHOLE,
        compiler_params=params(4),
        name="pair",
    )(mine, theirs)


def finish_kernel(*refs):
    *parts, free_in, own_ref, free_ref = refs
    half = own_ref.shape[0]
    d = lse([p[0:half, :] for p in parts])
    own_ref[...] = sum(p[half : 2 * half, :] for p in parts) - d
    free_ref[...] = free_in[...] - sum(p[2 * half : 2 * half + 1, 0:1] for p in parts)


def finish(parts, free):
    half = (parts[0].shape[0] - 8) // 2
    return pl.pallas_call(
        finish_kernel,
        out_shape=(jax.ShapeDtypeStruct((half, LANES), jnp.float32), jax.ShapeDtypeStruct(free.shape, jnp.float32)),
        in_specs=[WHOLE] * (len(parts) + 1),
        out_specs=(WHOLE, WHOLE),
        compiler_params=params(4),
        name="finish",
    )(*parts, free)


def join_kernel(mine_ref, theirs_ref, who_ref, out_ref):
    half = mine_ref.shape[0]
    even = (who_ref[...] & 1) == 0
    mine, theirs = mine_ref[...], theirs_ref[...]
    out_ref[0:half, :] = jnp.where(even, mine, theirs)
    out_ref[half:, :] = jnp.where(even, theirs, mine)


def join(mine, theirs, who):
    return pl.pallas_call(
        join_kernel,
        out_shape=jax.ShapeDtypeStruct((2 * mine.shape[0], LANES), jnp.float32),
        in_specs=[WHOLE] * 3,
        out_specs=WHOLE,
        compiler_params=params(4),
        name="join",
    )(mine, theirs, who)


def shift_state(value, size, move):
    return lax.ppermute(value, "state", [(i, move(i)) for i in range(size)])


def partner(value, size):
    return shift_state(value, size, lambda i: i ^ 1)


def others(value, size):
    return [
        shift_state(value, size, lambda i, d=d: (i + 2 * d) % size) for d in range(1, size // 2)
    ]


def shards(samp, state, energies, offsets, counts, labels):
    nk, width = energies.shape
    nblk = offsets.shape[1]
    mine = jnp.broadcast_to(lax.axis_index("state"), (1, 1)).astype(jnp.int32)
    *ex, offt, sums, local_label, who, counts_row = prep(
        energies, offsets, counts.reshape(1, nk), labels.reshape(nblk, width // nblk), mine
    )
    groups = nblk // GROUP
    cuts = [groups * step // ITERS for step in range(ITERS + 1)]
    picked = []
    for step in range(ITERS):
        pair = paired(sums, partner(sums, state), nblk)
        parts = [pair, *others(pair, state)]
        picked.append(pick(energies, local_label, cuts[step], cuts[step + 1] - cuts[step], pair))
        out = update(parts, ex, offt, samp, picked[-1:])
        gathered = lax.all_to_all(out, "samp", 0, 0, tiled=True)
        if step < ITERS - 1:
            sums = denom(gathered, counts_row, ex, offt)
    keep, send, free = denom(gathered, counts_row, ex, offt, (local_label, who, *picked))
    pair = paired(keep, partner(send, state), nblk // 2)
    own, free = finish([pair, *others(pair, state)], free)
    own = join(own, partner(own, state), who)
    return free.reshape(nk), own.reshape(width)


def solution(mesh):
    return jax.shard_map(
        functools.partial(shards, mesh.shape["samp"], mesh.shape["state"]),
        mesh=mesh,
        in_specs=(P("state", "samp"), P("state", "samp"), P("state"), P("samp")),
        out_specs=(P("state"), P("samp")),
        check_vma=False,
    )
```
